128 devices in a mesh: seq: 32 (over x, z, core), head: 4 (over y).
Axes of the slice: x: 4, y: 4, z: 4, core: 2. Of those that a mesh axis runs over, the one named last changes fastest.
Arguments:
- queries: bfloat16 [32768, 1024], P(('seq', 'head')), may hold values from -8 to 8
- keys: bfloat16 [32768, 1024], P(('seq', 'head')), may hold values from -8 to 8
- values: bfloat16 [32768, 1024], P(('seq', 'head')), may hold values from -6 to 6
- out_grad: bfloat16 [32768, 1024], P(('seq', 'head')), may hold values from -6 to 6
- random_blocks: int32 [256, 3], replicated, may hold values from 0 to 255, as said below
- global_blocks: int32 [2], replicated, may hold values from 0 to 255, as said below
Outputs:
- grad_queries: bfloat16 [32768, 1024], P(('seq', 'head'))
- grad_keys: bfloat16 [32768, 1024], P(('seq', 'head'))
- grad_values: bfloat16 [32768, 1024], P(('seq', 'head'))
The draws below stay inside these ranges and needn't reach their ends.
Inputs may be any that keep to these rules, and one draw needn't show every extreme that they name: `random_blocks`: row i lists the random key blocks of query block i; repeats may occur. Among the 24 entries of the rows of one index of seq (rows b with the same b // 8), at most 2 name blocks of any one index of seq; in every draw some index of seq is named exactly 2 times from every index. `global_blocks`: 2 different block numbers in any order; one of them is always the last block, 255.
All inputs are finite; a program needn't handle non-finite values.
Results may differ from the reference program's by a relative error of at most 0.006.
Values may be sent and summed in bfloat16 or wider, within the bound.
No kernel may reach another device: no remote copies, remote signals or barrier semaphores. Data moves between devices by JAX's collectives and lax.ppermute only.
A program may use at most 192 MiB of HBM per device.

```python
import math
import jax
import jax.numpy as jnp
from jax import lax

HEAD_DIM = 128
HEADS = 8
BLOCK = 128
GLOBAL = 2
RANDOM = 3
BLOCKS_DEV = 8
NBLOCKS = 256
TOKENS = 32768
CAP = 2
N_SEQ = 32


def draw_queries(key, part):
    key = jax.random.fold_in(key, 1)
    return jnp.clip(jax.random.normal(key, (TOKENS, HEADS * HEAD_DIM), jnp.float32), -8.0, 8.0).astype(jnp.bfloat16)


def draw_keys(key, part):
    key = jax.random.fold_in(key, 2)
    return jnp.clip(jax.random.normal(key, (TOKENS, HEADS * HEAD_DIM), jnp.float32), -8.0, 8.0).astype(jnp.bfloat16)


def draw_random_blocks(key, part):
    key = jax.random.fold_in(key, 5)
    hot_key, busy_key, score_key, order_key, local_key = jax.random.split(key, 5)
    tickets = N_SEQ * CAP
    requests = BLOCKS_DEV * RANDOM
    hot_owner = jax.random.randint(hot_key, (), 0, N_SEQ)
    busy_owner = jax.random.randint(busy_key, (N_SEQ,), 0, 4) == 0
    ticket_owner = jnp.arange(tickets) // CAP

    def one_sender(score_seed, order_seed):
        raw_score = jax.random.randint(score_seed, (tickets,), 0, 2 ** 20)
        raw_score = raw_score // jnp.where(busy_owner[ticket_owner], 4, 1)
        raw_score = jnp.where(ticket_owner == hot_owner, -1, raw_score)
        ranking = raw_score * tickets + jnp.arange(tickets)
        chosen = jnp.argsort(ranking)[:requests]
        owners = ticket_owner[chosen]
        return owners[jax.random.permutation(order_seed, requests)]
    owners = jax.vmap(one_sender)(jax.random.split(score_key, N_SEQ), jax.random.split(order_key, N_SEQ))
    local_block = jax.random.randint(local_key, (N_SEQ, requests), 0, BLOCKS_DEV)
    return (owners * BLOCKS_DEV + local_block).reshape(NBLOCKS, RANDOM).astype(jnp.int32)


def draw_global_blocks(key, part):
    key = jax.random.fold_in(key, 7)
    pick_key, order_key = jax.random.split(key)
    others = jax.random.permutation(pick_key, NBLOCKS - 1)[:GLOBAL - 1]
    listed = jnp.concatenate([others, jnp.full((1,), NBLOCKS - 1, others.dtype)])
    return listed[jax.random.permutation(order_key, GLOBAL)].astype(jnp.int32)


def steps_of(rng, shape, cuts, smallest, largest):
    level = 1.0
    for axis_at, parts in cuts:
        draws = jax.random.uniform(jax.random.fold_in(jax.random.fold_in(rng, 6), axis_at), (parts,), jnp.float32, smallest / len(cuts), largest / len(cuts))
        level = level * jnp.repeat(jnp.exp(draws), shape[axis_at] // parts).reshape((-1,) + (1,) * (len(shape) - 1 - axis_at))
    return level


def scatter_about(rng, dims, scale, bound, shards=(), kind=jnp.bfloat16):
    gain = steps_of(rng, dims, shards, -0.22, 0.18) if shards else 1.0
    values = jax.random.normal(rng, dims, jnp.float32) * scale * gain
    return jnp.minimum(jnp.maximum(values, -bound), bound).astype(kind)


def setup_inputs(seed: int = 0) -> dict:
    arg_keys = jax.random.split(jax.random.key(seed), 7)
    queries = draw_queries(jax.random.fold_in(arg_keys[6], 71), 0)
    keys = draw_keys(jax.random.fold_in(arg_keys[6], 71), 0)
    values = scatter_about(arg_keys[2], (TOKENS, HEADS * HEAD_DIM), 1.0, 6.0, ((0, 128),))
    out_grad = scatter_about(arg_keys[3], (TOKENS, HEADS * HEAD_DIM), 1.0, 6.0, ((0, 128),))
    random_blocks = draw_random_blocks(jax.random.fold_in(arg_keys[6], 71), 0)
    global_blocks = draw_global_blocks(jax.random.fold_in(arg_keys[6], 71), 0)
    return {"queries": queries, "keys": keys, "values": values, "out_grad": out_grad, "random_blocks": random_blocks, "global_blocks": global_blocks}


masked_score = -1e+30

def rounded(tensor):
    return lax.optimization_barrier(tensor.astype(jnp.bfloat16)).astype(jnp.float32)

def reference(queries, keys, values, out_grad, random_blocks, global_blocks):
    row_width = HEADS * HEAD_DIM
    score_scale = 1.0 / math.sqrt(HEAD_DIM)
    slot_count = 3 + GLOBAL + RANDOM
    local_slots = 3 + GLOBAL
    highest = lax.Precision.HIGHEST
    query_blocks = queries.reshape(NBLOCKS, BLOCK, HEADS, HEAD_DIM)
    grad_blocks = out_grad.reshape(NBLOCKS, BLOCK, HEADS, HEAD_DIM)
    pair_blocks = jnp.concatenate([keys, values], axis=1).reshape(NBLOCKS, BLOCK, 2 * row_width)

    def block_step(grad_sum, block_index):
        window_ids = jnp.stack([block_index - 1, block_index, block_index + 1]).astype(jnp.int32)
        entries = jnp.concatenate([window_ids, global_blocks.astype(jnp.int32), random_blocks[block_index].astype(jnp.int32)])
        present = jnp.concatenate([jnp.stack([block_index > 0, block_index >= 0, block_index < NBLOCKS - 1]), jnp.ones((GLOBAL + RANDOM,), bool)])
        clipped = jnp.clip(entries, 0, NBLOCKS - 1).astype(jnp.int32)
        chosen = jnp.take(pair_blocks, clipped, axis=0).reshape(slot_count * BLOCK, 2, HEADS, HEAD_DIM).astype(jnp.float32)
        keyset = chosen[:, 0]
        valset = chosen[:, 1]
        query_rows = query_blocks[block_index].astype(jnp.float32)
        grad_rows = grad_blocks[block_index].astype(jnp.float32)
        scores = jnp.einsum('thd,khd->htk', query_rows, keyset, precision=highest) * score_scale
        key_mask = jnp.repeat(present, BLOCK)
        scores = jnp.where(key_mask[None, None, :], scores, masked_score)
        row_max = lax.optimization_barrier(jnp.max(scores, axis=-1, keepdims=True))
        weights = jnp.exp(scores - row_max)
        row_probs = weights / lax.optimization_barrier(jnp.sum(weights, axis=-1, keepdims=True))
        prob_grad = jnp.einsum('thd,khd->htk', grad_rows, valset, precision=highest)
        row_delta = lax.optimization_barrier(jnp.sum(row_probs * prob_grad, axis=-1, keepdims=True))
        probs_low = rounded(row_probs)
        dscore = rounded(row_probs * (prob_grad - row_delta) * score_scale)
        dq_slots = jnp.einsum('htsk,skhd->sthd', dscore.reshape(HEADS, BLOCK, slot_count, BLOCK), keyset.reshape(slot_count, BLOCK, HEADS, HEAD_DIM), precision=highest)
        query_grad = lax.optimization_barrier(jnp.sum(dq_slots[:local_slots], axis=0)) + lax.optimization_barrier(jnp.sum(rounded(dq_slots[local_slots:]), axis=0))
        key_grad = jnp.einsum('htk,thd->khd', dscore, query_rows, precision=highest)
        value_grad = jnp.einsum('htk,thd->khd', probs_low, grad_rows, precision=highest)
        pair_terms = jnp.concatenate([key_grad.reshape(slot_count, BLOCK, row_width), value_grad.reshape(slot_count, BLOCK, row_width)], axis=-1)
        pair_terms = jnp.concatenate([pair_terms[:local_slots], rounded(pair_terms[local_slots:])], axis=0)
        zero_index = jnp.zeros((), jnp.int32)
        for slot_number in range(slot_count):
            where_at = (clipped[slot_number], zero_index, zero_index)
            current = lax.dynamic_slice(grad_sum, where_at, (1, BLOCK, 2 * row_width))
            grad_sum = lax.dynamic_update_slice(grad_sum, current + pair_terms[slot_number][None], where_at)
        return (grad_sum, query_grad.reshape(BLOCK, row_width).astype(jnp.bfloat16))
    grad_start = jnp.zeros((NBLOCKS, BLOCK, 2 * row_width), jnp.float32)
    grad_sum, dq_blocks = lax.scan(block_step, grad_start, jnp.arange(NBLOCKS, dtype=jnp.int32))
    pair_grads = grad_sum.astype(jnp.bfloat16).reshape(TOKENS, 2 * row_width)
    return (dq_blocks.reshape(TOKENS, row_width), pair_grads[:, :row_width], pair_grads[:, row_width:])
```

```python
import functools
import math

import jax
import jax.numpy as jnp
from jax import lax
from jax.experimental import pallas as pl
from jax.experimental.pallas import tpu as pltpu
from jax.sharding import PartitionSpec as P

HEAD_DIM = 128
BLOCK = 128
HEADS = 8
DEVICES = 128
OWN = 2
RANDOM = 3
GLOBAL = 2
ENTRIES = OWN * RANDOM + GLOBAL
TILE = 16
TILES = BLOCK // TILE
BLOCKS = DEVICES * OWN
AXES = ("seq", "head")
SCALE = 1.0 / math.sqrt(HEAD_DIM)
SCALE_LOG2 = SCALE * math.log2(math.e)
MASKED = -1e30
VMEM_LIMIT = 48 * 1024 * 1024


def params(**kw):
    return pltpu.CompilerParams(vmem_limit_bytes=VMEM_LIMIT, **kw)


def whole(shape):
    return pl.BlockSpec(shape, lambda *_: (0,) * len(shape))


def pack_kernel(k_ref, v_ref, tiles_ref, low_ref, high_ref):
    for part, ref in enumerate((k_ref, v_ref)):
        low_ref[pl.ds(part * BLOCK, BLOCK), :] = ref[:BLOCK, :]
        high_ref[pl.ds(part * BLOCK, BLOCK), :] = ref[BLOCK:, :]
        for head in range(HEADS):
            for block in range(OWN):
                tiles_ref[pl.ds((part * HEADS + head) * TILES, TILES), block] = ref[
                    pl.ds(block * BLOCK, BLOCK), pl.ds(head * HEAD_DIM, HEAD_DIM)
                ].reshape(TILES, TILE, HEAD_DIM)


def pack(keys, values):
    width = HEADS * HEAD_DIM
    edge = jax.ShapeDtypeStruct((2 * BLOCK, width), jnp.bfloat16)
    return pl.pallas_call(
        pack_kernel,
        out_shape=(
            jax.ShapeDtypeStruct((DEVICES, OWN, TILE, HEAD_DIM), jnp.bfloat16),
            edge,
            edge,
        ),
        compiler_params=params(),
        name="pack_tiles",
    )(keys, values)


def select_kernel(random_ref, global_ref, table_ref, out_ref):
    common = [table_ref[global_ref[which]] for which in range(GLOBAL)]

    def step(device, carry):
        for entry in range(OWN * RANDOM):
            out_ref[device, entry] = table_ref[random_ref[device * (OWN * RANDOM) + entry]]
        for which in range(GLOBAL):
            out_ref[device, OWN * RANDOM + which] = common[which]
        return carry

    lax.fori_loop(0, DEVICES, step, 0, unroll=4)


def select(random_list, global_blocks, table):
    shape = (DEVICES, ENTRIES, TILE, HEAD_DIM)
    return pl.pallas_call(
        select_kernel,
        grid_spec=pltpu.PrefetchScalarGridSpec(
            num_scalar_prefetch=2,
            grid=(1,),
            in_specs=[whole(table.shape)],
            out_specs=whole(shape),
        ),
        out_shape=jax.ShapeDtypeStruct(shape, jnp.bfloat16),
        compiler_params=params(),
        name="select_tiles",
    )(random_list, global_blocks, table)


def dot_nt(a, b):
    return lax.dot_general(a, b, (((1,), (1,)), ((), ())), preferred_element_type=jnp.float32)


def dot_nn(a, b):
    return lax.dot_general(a, b, (((1,), (0,)), ((), ())), preferred_element_type=jnp.float32)


def dot_tn(a, b):
    return lax.dot_general(a, b, (((0,), (0,)), ((), ())), preferred_element_type=jnp.float32)


def attend_kernel(
    device_ref, q_ref, d_ref, k_ref, v_ref, prev_ref, next_ref, far_ref,
    dq_ref, wk_ref, wv_ref, to_prev_ref, to_next_ref, terms_ref,
):
    device = device_ref[0]
    queries = q_ref[...]
    grads = d_ref[...]

    def entry(part, index):
        return far_ref[part, 0, :, index].reshape(BLOCK, HEAD_DIM)

    def keyset(part, own_ref):
        shared = jnp.concatenate(
            [own_ref[...], entry(part, OWN * RANDOM), entry(part, OWN * RANDOM + 1)], axis=0
        )
        private = []
        for block, edge in enumerate((prev_ref, next_ref)):
            private.append(
                jnp.concatenate(
                    [edge[pl.ds(part * BLOCK, BLOCK), :]]
                    + [entry(part, block * RANDOM + r) for r in range(RANDOM)],
                    axis=0,
                )
            )
        return shared, private

    def rows(block):
        return slice(block * BLOCK, (block + 1) * BLOCK)

    k_shared, k_private = keyset(0, k_ref)
    v_shared, v_private = keyset(1, v_ref)

    s_shared = dot_nt(k_shared, queries) * SCALE_LOG2
    s_private = (
        jnp.concatenate([dot_nt(k_private[b], queries[rows(b)]) for b in range(OWN)], axis=1)
        * SCALE_LOG2
    )
    column = lax.broadcasted_iota(jnp.int32, (1, OWN * BLOCK), 1)
    absent = ((column < BLOCK) & (device == 0)) | ((column >= BLOCK) & (device == DEVICES - 1))
    s_edge = jnp.where(absent, MASKED, s_private[:BLOCK])
    s_random = s_private[BLOCK:]
    p_shared = dot_nt(v_shared, grads)
    p_private = jnp.concatenate(
        [dot_nt(v_private[b], grads[rows(b)]) for b in range(OWN)], axis=1
    )
    row_max = jnp.maximum(
        jnp.maximum(
            jnp.max(s_shared, axis=0, keepdims=True), jnp.max(s_edge, axis=0, keepdims=True)
        ),
        jnp.max(s_random, axis=0, keepdims=True),
    )
    e_shared = jnp.exp2(s_shared - row_max)
    e_private = jnp.concatenate([jnp.exp2(s_edge - row_max), jnp.exp2(s_random - row_max)], axis=0)
    total = jnp.sum(e_shared, axis=0, keepdims=True) + jnp.sum(e_private, axis=0, keepdims=True)
    inverse = 1.0 / total
    delta = (
        jnp.sum(e_shared * p_shared, axis=0, keepdims=True)
        + jnp.sum(e_private * p_private, axis=0, keepdims=True)
    ) * inverse

    probs_shared = e_shared * inverse
    probs_private = e_private * inverse
    low_shared = probs_shared.astype(jnp.bfloat16)
    low_private = probs_private.astype(jnp.bfloat16)
    ds_shared = (probs_shared * ((p_shared - delta) * SCALE)).astype(jnp.bfloat16)
    ds_private = (probs_private * ((p_private - delta) * SCALE)).astype(jnp.bfloat16)

    dq_shared = dot_tn(k_shared, ds_shared)
    dq_private = jnp.concatenate(
        [dot_tn(k_private[b], ds_private[:, rows(b)]) for b in range(OWN)], axis=1
    )
    dq_ref[...] = (dq_shared + dq_private).T.astype(jnp.bfloat16)

    for part, weights_shared, weights_private, other, own_ref in (
        (0, ds_shared, ds_private, queries, wk_ref),
        (1, low_shared, low_private, grads, wv_ref),
    ):
        shared = dot_nn(weights_shared, other)
        own_ref[...] = shared[: OWN * BLOCK]
        for which in range(GLOBAL):
            terms_ref[part, 0, :, OWN * RANDOM + which] = (
                shared[rows(OWN + which)].astype(jnp.bfloat16).reshape(TILES, TILE, HEAD_DIM)
            )
        for block, edge in enumerate((to_prev_ref, to_next_ref)):
            private = dot_nn(weights_private[:, rows(block)], other[rows(block)]).astype(
                jnp.bfloat16
            )
            edge[pl.ds(part * BLOCK, BLOCK), :] = private[:BLOCK]
            for r in range(RANDOM):
                terms_ref[part, 0, :, block * RANDOM + r] = private[rows(1 + r)].reshape(
                    TILES, TILE, HEAD_DIM
                )


def attend(device, queries, grads, keys, values, from_prev, from_next, far):
    width = HEADS * HEAD_DIM
    rows = OWN * BLOCK
    far_shape = (2, HEADS, TILES, ENTRIES, TILE, HEAD_DIM)
    column = pl.BlockSpec((rows, HEAD_DIM), lambda h, *_: (0, h))
    far_spec = pl.BlockSpec((2, 1, TILES, ENTRIES, TILE, HEAD_DIM), lambda h, *_: (0, h, 0, 0, 0, 0))
    low = jax.ShapeDtypeStruct((rows, width), jnp.bfloat16)
    high = jax.ShapeDtypeStruct((rows, width), jnp.float32)
    return pl.pallas_call(
        attend_kernel,
        grid_spec=pltpu.PrefetchScalarGridSpec(
            num_scalar_prefetch=1,
            grid=(HEADS,),
            in_specs=[column] * 6 + [far_spec],
            out_specs=[column] * 5 + [far_spec],
        ),
        out_shape=(low, high, high, low, low, jax.ShapeDtypeStruct(far_shape, jnp.bfloat16)),
        compiler_params=params(),
        name="attend",
    )(device, queries, grads, keys, values, from_prev, from_next, far.reshape(far_shape))


def collect_kernel(random_ref, global_ref, terms_ref, out_ref, *sums):
    for sum_ref in sums:
        sum_ref[...] = jnp.zeros_like(sum_ref)

    def step(device, carry):
        for entry in range(OWN * RANDOM):
            sum_ref = sums[entry % len(sums)]
            block = random_ref[device * (OWN * RANDOM) + entry]
            sum_ref[block] = sum_ref[block] + terms_ref[device, entry].astype(jnp.float32)
        return tuple(
            carry[which] + terms_ref[device, OWN * RANDOM + which].astype(jnp.float32)
            for which in range(GLOBAL)
        )

    zero = jnp.zeros((TILE, HEAD_DIM), jnp.float32)
    totals = lax.fori_loop(0, DEVICES, step, (zero,) * GLOBAL, unroll=2)
    for which in range(GLOBAL):
        block = global_ref[which]
        sums[0][block] = sums[0][block] + totals[which]
    result = sums[0][...]
    for sum_ref in sums[1:]:
        result = result + sum_ref[...]
    out_ref[...] = result.astype(jnp.bfloat16)


def collect(random_list, global_blocks, terms):
    shape = (BLOCKS, TILE, HEAD_DIM)
    return pl.pallas_call(
        collect_kernel,
        grid_spec=pltpu.PrefetchScalarGridSpec(
            num_scalar_prefetch=2,
            grid=(1,),
            in_specs=[whole(terms.shape)],
            out_specs=whole(shape),
            scratch_shapes=[pltpu.VMEM(shape, jnp.float32)] * 3,
        ),
        out_shape=jax.ShapeDtypeStruct(shape, jnp.bfloat16),
        compiler_params=params(),
        name="collect_terms",
    )(random_list, global_blocks, terms)


def finish_kernel(wk_ref, wv_ref, prev_ref, next_ref, far_ref, dk_ref, dv_ref):
    for part, (own_ref, out_ref) in enumerate(((wk_ref, dk_ref), (wv_ref, dv_ref))):
        for block, edge in enumerate((prev_ref, next_ref)):
            rows = pl.ds(block * BLOCK, BLOCK)
            far = far_ref[part, 0, :, block].reshape(BLOCK, HEAD_DIM).astype(jnp.float32)
            near = edge[pl.ds(part * BLOCK, BLOCK), :].astype(jnp.float32)
            out_ref[rows, :] = (own_ref[rows, :] + near + far).astype(jnp.bfloat16)


def finish(wk, wv, from_prev, from_next, far):
    width = HEADS * HEAD_DIM
    rows = OWN * BLOCK
    far_shape = (2, HEADS, TILES, OWN, TILE, HEAD_DIM)
    column = pl.BlockSpec((rows, HEAD_DIM), lambda h: (0, h))
    low = jax.ShapeDtypeStruct((rows, width), jnp.bfloat16)
    return pl.pallas_call(
        finish_kernel,
        grid=(HEADS,),
        in_specs=[column] * 4
        + [pl.BlockSpec((2, 1, TILES, OWN, TILE, HEAD_DIM), lambda h: (0, h, 0, 0, 0, 0))],
        out_specs=[column] * 2,
        out_shape=(low, low),
        compiler_params=params(),
        name="finish",
    )(wk, wv, from_prev, from_next, far.reshape(far_shape))


def exchange(tiles):
    return lax.all_to_all(tiles, AXES, split_axis=0, concat_axis=0, tiled=True)


UP = [(i, i + 1) for i in range(DEVICES - 1)]
DOWN = [(i + 1, i) for i in range(DEVICES - 1)]


def local(queries, keys, values, out_grad, random_blocks, global_blocks):
    device = lax.axis_index(AXES).astype(jnp.int32).reshape(1)
    random_list = random_blocks.reshape(-1)
    tiles, low, high = pack(keys, values)
    from_prev = lax.ppermute(high, AXES, UP)
    from_next = lax.ppermute(low, AXES, DOWN)
    table = exchange(tiles).reshape(BLOCKS, TILE, HEAD_DIM)
    far = exchange(select(random_list, global_blocks, table))
    dq, wk, wv, to_prev, to_next, terms = attend(
        device, queries, out_grad, keys, values, from_prev, from_next, far
    )
    grad_from_next = lax.ppermute(to_prev, AXES, DOWN)
    grad_from_prev = lax.ppermute(to_next, AXES, UP)
    returned = exchange(terms.reshape(DEVICES, ENTRIES, TILE, HEAD_DIM))
    sums = collect(random_list, global_blocks, returned)
    back = exchange(sums.reshape(DEVICES, OWN, TILE, HEAD_DIM))
    dk, dv = finish(wk, wv, grad_from_prev, grad_from_next, back)
    return dq, dk, dv


def solution(mesh):
    split = P(AXES, None)
    return jax.shard_map(
        local,
        mesh=mesh,
        in_specs=(split, split, split, split, P(), P()),
        out_specs=(split, split, split),
        check_vma=False,
    )
```

```python
import math

import jax
import jax.numpy as jnp
from jax import lax
from jax.experimental import pallas as pl
from jax.experimental.pallas import tpu as pltpu
from jax.sharding import PartitionSpec as P

HEAD_DIM = 128
BLOCK = 128
HEADS = 8
SEQ = 32
GROUPS = 4
PAIR = HEADS // GROUPS
DEVICES = SEQ * GROUPS
OWN = 2
LOCAL = OWN * GROUPS
RANDOM = 3
GLOBAL = 2
STEP = OWN * RANDOM
ASKED = LOCAL * RANDOM
ENTRIES = ASKED + GLOBAL
RETURNED = ENTRIES + 2
TILE = 16
TILES = BLOCK // TILE
BLOCKS = SEQ * LOCAL
ROWS = OWN * BLOCK
TOKENS = LOCAL * BLOCK
WIDTH = HEADS * HEAD_DIM
COLS = PAIR * HEAD_DIM
AXES = ("seq", "head")
SCALE = 1.0 / math.sqrt(HEAD_DIM)
SCALE_LOG2 = SCALE * math.log2(math.e)
MASKED = -1e30
VMEM_LIMIT = 24 * 1024 * 1024
WIDE_LIMIT = 56 * 1024 * 1024
SELECT_LIMIT = 50 * 1024 * 1024
ATTEND_LIMIT = 46 * 1024 * 1024
LOW = jnp.bfloat16


def shape_of(shape, kind=LOW):
    return jax.ShapeDtypeStruct(shape, kind)


INSIDE = pl.BlockSpec(memory_space=pltpu.VMEM)
OUTSIDE = pl.BlockSpec(memory_space=pl.ANY)


def call(kernel, name, scalars, arrays, outs, scratch=(), far_in=(), far_out=(), limit=VMEM_LIMIT):
    return pl.pallas_call(
        kernel,
        in_specs=[pl.BlockSpec(memory_space=pltpu.SMEM)] * len(scalars)
        + [OUTSIDE if i in far_in else INSIDE for i in range(len(arrays))],
        out_specs=tuple(OUTSIDE if i in far_out else INSIDE for i in range(len(outs))),
        out_shape=tuple(outs),
        scratch_shapes=list(scratch),
        compiler_params=pltpu.CompilerParams(vmem_limit_bytes=limit),
        name=name,
    )(*scalars, *arrays)


def group_columns(group):
    return pl.ds(pl.multiple_of(group * COLS, COLS), COLS)


def group_rows(group):
    return pl.ds(pl.multiple_of(group * ROWS, ROWS), ROWS)


def pack_kernel(k_ref, v_ref, tiles_ref, rows_ref, packed_ref, in_sems, out_sems):
    def fetch(part, block):
        rows = pl.ds(block * BLOCK, BLOCK)
        return pltpu.make_async_copy(
            (k_ref, v_ref)[part].at[rows, :], rows_ref.at[part, block], in_sems.at[part, block]
        )

    def ship(part, parity):
        return pltpu.make_async_copy(
            packed_ref.at[part, parity], tiles_ref.at[part, parity], out_sems.at[part, parity]
        )

    for part in range(2):
        for block in range(OWN):
            fetch(part, block).start()
    for part in range(2):
        for block in range(OWN):
            fetch(part, block).wait()
        for parity in range(PAIR):
            for group in range(GROUPS):
                for block in range(OWN):
                    packed_ref[part, parity, :, group, block] = rows_ref[
                        part, block, :, pl.ds((group * PAIR + parity) * HEAD_DIM, HEAD_DIM)
                    ].reshape(TILES, TILE, HEAD_DIM)
            ship(part, parity).start()
    for part in range(2):
        for parity in range(PAIR):
            ship(part, parity).wait()


def split_kernel(group_ref, *refs):
    for distance in range(GROUPS):
        columns = group_columns((group_ref[0] + distance) % GROUPS)
        for which in range(4):
            refs[4 + distance][which] = refs[which][:, columns]


def assemble_kernel(group_ref, *refs):
    near_ref, low_ref, high_ref = refs[GROUPS:]
    for distance in range(GROUPS):
        rows = group_rows((group_ref[0] + GROUPS - distance) % GROUPS)
        for which in range(4):
            near_ref[which, rows, :] = refs[distance][which]
    for part in range(2):
        low_ref[part] = near_ref[2 + part, :BLOCK, :]
        high_ref[part] = near_ref[2 + part, TOKENS - BLOCK :, :]


CHUNK = 4


def select_kernel(random_ref, global_ref, table_ref, out_ref, chosen_ref, sems):
    common = [table_ref[global_ref[which]] for which in range(GLOBAL)]

    def ship(chunk):
        part = pl.ds(chunk * CHUNK, CHUNK)
        return pltpu.make_async_copy(chosen_ref.at[part], out_ref.at[part], sems.at[chunk])

    def fill(chunk, carry):
        for device in range(CHUNK):
            place = chunk * CHUNK + device
            for entry in range(ASKED):
                chosen_ref[place, entry] = table_ref[random_ref[place * ASKED + entry]]
            for which in range(GLOBAL):
                chosen_ref[place, ASKED + which] = common[which]
        ship(chunk).start()
        return carry

    def drain(chunk, carry):
        ship(chunk).wait()
        return carry

    lax.fori_loop(0, SEQ // CHUNK, fill, 0)
    lax.fori_loop(0, SEQ // CHUNK, drain, 0)


def dot_nt(a, b):
    return lax.dot_general(a, b, (((1,), (1,)), ((), ())), preferred_element_type=jnp.float32)


def dot_nn(a, b):
    return lax.dot_general(a, b, (((1,), (0,)), ((), ())), preferred_element_type=jnp.float32)


def dot_tn(a, b):
    return lax.dot_general(a, b, (((0,), (0,)), ((), ())), preferred_element_type=jnp.float32)


def rows_of(block):
    return slice(block * BLOCK, (block + 1) * BLOCK)


def columns_of(head):
    return pl.ds(head * HEAD_DIM, HEAD_DIM)


def step_rows(step):
    return pl.ds(pl.multiple_of(step * ROWS, ROWS), ROWS)


def edge_block(step, head, part, own_ref, prev_ref, next_ref, block):
    columns = columns_of(head)
    if block == 0:
        index = jnp.maximum(OWN * step - 1, 0)
        absent, outer = step == 0, prev_ref
    else:
        index = jnp.minimum(OWN * step + OWN, LOCAL - 1)
        absent, outer = step == GROUPS - 1, next_ref
    rows = pl.ds(pl.multiple_of(index * BLOCK, BLOCK), BLOCK)
    return jnp.where(absent, outer[part, :, columns], own_ref[rows, columns])


def keysets(step, head, part, own_ref, prev_ref, next_ref, far_ref):
    def entry(index):
        return far_ref[part, head, :, index].reshape(BLOCK, HEAD_DIM)

    shared = jnp.concatenate(
        [own_ref[step_rows(step), columns_of(head)]]
        + [entry(ASKED + which) for which in range(GLOBAL)],
        axis=0,
    )
    private = [
        jnp.concatenate(
            [edge_block(step, head, part, own_ref, prev_ref, next_ref, block)]
            + [entry(step * STEP + block * RANDOM + r) for r in range(RANDOM)],
            axis=0,
        )
        for block in range(OWN)
    ]
    return shared, private


def to_tiles(block):
    return block.astype(LOW).reshape(TILES, TILE, HEAD_DIM)


SAVED = (GROUPS, PAIR, 6 * ROWS + BLOCK, ROWS)


def saved_parts(ref):
    return ref.at[:, :, : 4 * ROWS, :], ref.at[:, :, 4 * ROWS :, :]


def attend_kernel(
    place_ref, near_ref, prev_ref, next_ref, far_ref,
    terms_out, saved_out,
    terms_ref, saved_ref, term_sems, out_sems,
):
    place = place_ref[0]
    q_ref, d_ref, k_ref, v_ref = (near_ref.at[which] for which in range(4))
    ds_ref, low_ref = saved_parts(saved_ref)

    def ship_terms(index, start, size):
        entries = pl.ds(start, size)
        return pltpu.make_async_copy(
            terms_ref.at[:, :, :, entries], terms_out.at[:, :, :, entries], term_sems.at[index]
        )

    def ship(step):
        return [
            pltpu.make_async_copy(saved_ref.at[step], saved_out.at[step], out_sems.at[step]),
            ship_terms(step, step * STEP, STEP),
        ]

    column = lax.broadcasted_iota(jnp.int32, (1, ROWS), 1)

    def attend_head(step, head):
        queries = q_ref[step_rows(step), columns_of(head)]
        grads = d_ref[step_rows(step), columns_of(head)]
        k_shared, k_private = keysets(step, head, 0, k_ref, prev_ref, next_ref, far_ref)
        v_shared, v_private = keysets(step, head, 1, v_ref, prev_ref, next_ref, far_ref)

        s_shared = dot_nt(k_shared, queries) * SCALE_LOG2
        s_private = (
            jnp.concatenate([dot_nt(k_private[b], queries[rows_of(b)]) for b in range(OWN)], axis=1)
            * SCALE_LOG2
        )
        absent = ((column < BLOCK) & (step == 0) & (place == 0)) | (
            (column >= BLOCK) & (step == GROUPS - 1) & (place == SEQ - 1)
        )
        s_edge = jnp.where(absent, MASKED, s_private[:BLOCK])
        s_random = s_private[BLOCK:]
        p_shared = dot_nt(v_shared, grads)
        p_private = jnp.concatenate(
            [dot_nt(v_private[b], grads[rows_of(b)]) for b in range(OWN)], axis=1
        )
        row_max = jnp.maximum(
            jnp.maximum(
                jnp.max(s_shared, axis=0, keepdims=True), jnp.max(s_edge, axis=0, keepdims=True)
            ),
            jnp.max(s_random, axis=0, keepdims=True),
        )
        e_shared = jnp.exp2(s_shared - row_max)
        e_private = jnp.concatenate(
            [jnp.exp2(s_edge - row_max), jnp.exp2(s_random - row_max)], axis=0
        )
        total = jnp.sum(e_shared, axis=0, keepdims=True) + jnp.sum(
            e_private, axis=0, keepdims=True
        )
        inverse = 1.0 / total
        delta = (
            jnp.sum(e_shared * p_shared, axis=0, keepdims=True)
            + jnp.sum(e_private * p_private, axis=0, keepdims=True)
        ) * inverse

        probs_shared = e_shared * inverse
        probs_private = e_private * inverse
        low_private = probs_private.astype(LOW)
        ds_private = (probs_private * ((p_private - delta) * SCALE)).astype(LOW)
        low_ref[step, head, : 2 * ROWS, :] = probs_shared.astype(LOW)
        low_ref[step, head, 2 * ROWS :, :] = low_private[:BLOCK]
        ds_ref[step, head, : 2 * ROWS, :] = (
            probs_shared * ((p_shared - delta) * SCALE)
        ).astype(LOW)
        ds_ref[step, head, 2 * ROWS :, :] = ds_private

        for part, weights, other in ((0, ds_private, queries), (1, low_private, grads)):
            for block in range(OWN):
                terms = dot_nn(weights[BLOCK:, rows_of(block)], other[rows_of(block)])
                for r in range(RANDOM):
                    terms_ref[part, head, :, step * STEP + block * RANDOM + r] = to_tiles(
                        terms[rows_of(r)]
                    )

    for step in range(GROUPS):
        for head in range(PAIR):
            attend_head(step, head)
        for copy in ship(step):
            copy.start()
    for part, weights_ref, other_ref in ((0, ds_ref, q_ref), (1, low_ref, d_ref)):
        for head in range(PAIR):
            total = sum(
                dot_nn(
                    weights_ref[step, head, ROWS : 2 * ROWS, :],
                    other_ref[pl.ds(step * ROWS, ROWS), columns_of(head)],
                )
                for step in range(GROUPS)
            )
            for which in range(GLOBAL):
                terms_ref[part, head, :, ASKED + which] = to_tiles(total[rows_of(which)])
            for block, step in enumerate((0, GROUPS - 1)):
                terms_ref[part, head, :, ENTRIES + block] = to_tiles(
                    dot_nn(
                        weights_ref[step, head, 2 * ROWS : 2 * ROWS + BLOCK, rows_of(block)],
                        other_ref[
                            pl.ds(step * ROWS + block * BLOCK, BLOCK), columns_of(head)
                        ],
                    )
                )
    last = ship_terms(GROUPS, ASKED, RETURNED - ASKED)
    last.start()
    for step in range(GROUPS):
        for copy in ship(step):
            copy.wait()
    last.wait()


def attend(place, near, from_prev, from_next, far):
    terms_shape = (2, PAIR, TILES, RETURNED, TILE, HEAD_DIM)
    return call(
        attend_kernel,
        "attend",
        [place],
        [near, from_prev, from_next, far.reshape((2, PAIR, TILES, ENTRIES, TILE, HEAD_DIM))],
        [shape_of(terms_shape), shape_of(SAVED)],
        [
            pltpu.VMEM(terms_shape, LOW),
            pltpu.VMEM(SAVED, LOW),
            pltpu.SemaphoreType.DMA((GROUPS + 1,)),
            pltpu.SemaphoreType.DMA((GROUPS,)),
        ],
        far_out=(0, 1),
        limit=ATTEND_LIMIT,
    )


def near_kernel(
    near_ref, prev_ref, next_ref, far_ref, saved_ref, dq_ref, win_ref, sum_ref
):
    ds_ref, low_ref = saved_parts(saved_ref)
    q_ref, d_ref, k_ref = (near_ref.at[which] for which in range(3))
    sum_ref[...] = jnp.zeros_like(sum_ref)

    def near_head(step, head):
        columns = columns_of(head)
        k_shared, k_private = keysets(step, head, 0, k_ref, prev_ref, next_ref, far_ref)
        dq_shared = dot_tn(k_shared, ds_ref[step, head, : 2 * ROWS, :])
        dq_private = jnp.concatenate(
            [
                dot_tn(k_private[b], ds_ref[step, head, 2 * ROWS :, rows_of(b)])
                for b in range(OWN)
            ],
            axis=1,
        )
        dq_ref[step_rows(step), columns] = (dq_shared + dq_private).T.astype(LOW)
        start = pl.multiple_of(step * ROWS, ROWS)
        for part, weights_ref, other_ref in ((0, ds_ref, q_ref), (1, low_ref, d_ref)):
            other = other_ref[step_rows(step), columns]
            own = pl.ds(start + BLOCK, ROWS)
            sum_ref[part, own, columns] = sum_ref[part, own, columns] + dot_nn(
                weights_ref[step, head, :ROWS, :], other
            )
            for block in range(OWN):
                edge = pl.ds(start + block * (BLOCK + ROWS), BLOCK)
                sum_ref[part, edge, columns] = sum_ref[part, edge, columns] + dot_nn(
                    weights_ref[step, head, 2 * ROWS : 2 * ROWS + BLOCK, rows_of(block)],
                    other[rows_of(block)],
                )

    def body(step, carry):
        for head in range(PAIR):
            near_head(step, head)
        return carry

    lax.fori_loop(0, GROUPS, body, 0)
    for part in range(2):
        win_ref[part] = sum_ref[part, BLOCK : BLOCK + TOKENS, :]


def near_grads(near, from_prev, from_next, far, saved):
    return call(
        near_kernel,
        "near_grads",
        [],
        [
            near, from_prev, from_next,
            far.reshape((2, PAIR, TILES, ENTRIES, TILE, HEAD_DIM)), saved,
        ],
        [
            shape_of((TOKENS, COLS)),
            shape_of((2, TOKENS, COLS), jnp.float32),
        ],
        [pltpu.VMEM((2, TOKENS + 2 * BLOCK, COLS), jnp.float32)],
    )


def collect_kernel(random_ref, global_ref, terms_in, out_ref, terms_ref, sems, *sums):
    def fetch(chunk):
        part = pl.ds(chunk * CHUNK, CHUNK)
        return pltpu.make_async_copy(terms_in.at[part], terms_ref.at[part], sems.at[chunk])

    def begin(chunk, carry):
        fetch(chunk).start()
        return carry

    lax.fori_loop(0, SEQ // CHUNK, begin, 0)
    for sum_ref in sums:
        sum_ref[...] = jnp.zeros_like(sum_ref)

    def add(which, block, device, entry):
        sum_ref = sums[which % len(sums)]
        sum_ref[block] = sum_ref[block] + terms_ref[device, entry].astype(jnp.float32)

    def step(chunk, carry):
        fetch(chunk).wait()
        for inner in range(CHUNK):
            device = chunk * CHUNK + inner
            for entry in range(ASKED):
                add(entry, random_ref[device * ASKED + entry], device, entry)
            add(0, jnp.maximum(device * LOCAL - 1, 0), device, ENTRIES)
            add(1, jnp.minimum(device * LOCAL + LOCAL, BLOCKS - 1), device, ENTRIES + 1)
            carry = tuple(
                carry[which] + terms_ref[device, ASKED + which].astype(jnp.float32)
                for which in range(GLOBAL)
            )
        return carry

    zero = jnp.zeros((TILE, HEAD_DIM), jnp.float32)
    totals = lax.fori_loop(0, SEQ // CHUNK, step, (zero,) * GLOBAL)
    for which in range(GLOBAL):
        block = global_ref[which]
        sums[0][block] = sums[0][block] + totals[which]
    result = sums[0][...]
    for sum_ref in sums[1:]:
        result = result + sum_ref[...]
    out_ref[...] = result.astype(LOW)


def regroup_kernel(group_ref, dq_ref, win_ref, *outs):
    for distance, out_ref in enumerate(outs):
        rows = group_rows((group_ref[0] + distance) % GROUPS)
        out_ref[0] = dq_ref[rows, :]
        for part in range(2):
            out_ref[1 + part] = win_ref[part, rows, :].astype(LOW)


def finish_kernel(group_ref, *refs):
    far_ref, dq_ref, dk_ref, dv_ref = refs[GROUPS:]
    for distance in range(GROUPS):
        group = (group_ref[0] + GROUPS - distance) % GROUPS
        near_ref = refs[distance]
        dq_ref[:, group_columns(group)] = near_ref[0]
        for part, out_ref in enumerate((dk_ref, dv_ref)):
            for parity in range(PAIR):
                columns = pl.ds(
                    pl.multiple_of(group * COLS + parity * HEAD_DIM, HEAD_DIM), HEAD_DIM
                )
                for block in range(OWN):
                    rows = pl.ds(block * BLOCK, BLOCK)
                    far = far_ref[part, parity, :, group, block].reshape(BLOCK, HEAD_DIM)
                    near = near_ref[1 + part, rows, pl.ds(parity * HEAD_DIM, HEAD_DIM)]
                    out_ref[rows, columns] = (
                        near.astype(jnp.float32) + far.astype(jnp.float32)
                    ).astype(LOW)


def exchange(tiles, axes):
    return lax.all_to_all(tiles, axes, split_axis=0, concat_axis=0, tiled=True)


def around(parts):
    moved = [parts[0]]
    for distance in range(1, GROUPS):
        route = [(i, (i + distance) % GROUPS) for i in range(GROUPS)]
        moved.append(lax.ppermute(parts[distance], "head", route))
    return moved


def beside(up, down):
    forward = [(i, i + 1) for i in range(SEQ - 1)]
    backward = [(i + 1, i) for i in range(SEQ - 1)]
    return lax.ppermute(up, "seq", forward), lax.ppermute(down, "seq", backward)


def local(queries, keys, values, out_grad, random_blocks, global_blocks):
    place = lax.axis_index("seq").astype(jnp.int32).reshape(1)
    group = lax.axis_index("head").astype(jnp.int32).reshape(1)
    random_list = random_blocks.reshape(-1)
    tile_shape = (2, PAIR, TILES, GROUPS, OWN, TILE, HEAD_DIM)

    (tiles,) = call(
        pack_kernel,
        "pack_tiles",
        [],
        [keys, values],
        [shape_of(tile_shape)],
        [
            pltpu.VMEM((2, OWN, BLOCK, WIDTH), LOW),
            pltpu.VMEM(tile_shape, LOW),
            pltpu.SemaphoreType.DMA((2, OWN)),
            pltpu.SemaphoreType.DMA((2, PAIR)),
        ],
        far_in=(0, 1),
        far_out=(0,),
        limit=WIDE_LIMIT,
    )
    table = exchange(tiles.reshape(DEVICES, OWN, TILE, HEAD_DIM), AXES)
    split = call(
        split_kernel,
        "split_heads",
        [group],
        [queries, out_grad, keys, values],
        [shape_of((4, ROWS, COLS))] * GROUPS,
    )
    table, *split = lax.optimization_barrier((table, *split))
    edge_shape = shape_of((2, BLOCK, COLS))
    here, low, high = call(
        assemble_kernel,
        "assemble_heads",
        [group],
        around(split),
        [shape_of((4, TOKENS, COLS))] + [edge_shape] * 2,
    )
    from_prev, from_next = beside(high, low)
    (chosen,) = call(
        select_kernel,
        "select_tiles",
        [random_list, global_blocks],
        [table.reshape(BLOCKS, TILE, HEAD_DIM)],
        [shape_of((SEQ, ENTRIES, TILE, HEAD_DIM))],
        [
            pltpu.VMEM((SEQ, ENTRIES, TILE, HEAD_DIM), LOW),
            pltpu.SemaphoreType.DMA((SEQ // CHUNK,)),
        ],
        far_out=(0,),
        limit=SELECT_LIMIT,
    )
    far = exchange(chosen, "seq")
    terms, saved = attend(
        place, here, from_prev, from_next, far
    )
    returned = exchange(terms.reshape(SEQ, RETURNED, TILE, HEAD_DIM), "seq")
    dq, win = near_grads(
        here, from_prev, from_next, far, saved
    )
    back_parts = call(
        regroup_kernel,
        "regroup",
        [group],
        [dq, win],
        [shape_of((3, ROWS, COLS))] * GROUPS,
    )
    near = around(back_parts)
    returned, *near = lax.optimization_barrier((returned, *near))
    (sums,) = call(
        collect_kernel,
        "collect_terms",
        [random_list, global_blocks],
        [returned],
        [shape_of((BLOCKS, TILE, HEAD_DIM))],
        [
            pltpu.VMEM((SEQ, RETURNED, TILE, HEAD_DIM), LOW),
            pltpu.SemaphoreType.DMA((SEQ // CHUNK,)),
        ]
        + [pltpu.VMEM((BLOCKS, TILE, HEAD_DIM), jnp.float32)] * 3,
        far_in=(0,),
        limit=VMEM_LIMIT,
    )
    back = exchange(sums.reshape(DEVICES, OWN, TILE, HEAD_DIM), AXES)
    return call(
        finish_kernel,
        "finish",
        [group],
        list(near) + [back.reshape(tile_shape)],
        [shape_of((ROWS, WIDTH))] * 3,
    )


def solution(mesh):
    split = P(AXES, None)
    return jax.shard_map(
        local,
        mesh=mesh,
        in_specs=(split, split, split, split, P(), P()),
        out_specs=(split, split, split),
        check_vma=False,
    )
```

```python
import math

import jax
import jax.numpy as jnp
from jax import lax
from jax.experimental import pallas as pl
from jax.experimental.pallas import tpu as pltpu
from jax.sharding import PartitionSpec as P

HEAD_DIM = 128
BLOCK = 128
HEADS = 8
SEQ = 32
GROUPS = 4
PAIR = HEADS // GROUPS
DEVICES = SEQ * GROUPS
OWN = 2
LOCAL = OWN * GROUPS
RANDOM = 3
GLOBAL = 2
STEP = OWN * RANDOM
ASKED = LOCAL * RANDOM
ENTRIES = ASKED + GLOBAL
RETURNED = ENTRIES + 2
TILE = 16
TILES = BLOCK // TILE
BLOCKS = SEQ * LOCAL
ROWS = OWN * BLOCK
TOKENS = LOCAL * BLOCK
WIDTH = HEADS * HEAD_DIM
COLS = PAIR * HEAD_DIM
AXES = ("seq", "head")
SCALE = 1.0 / math.sqrt(HEAD_DIM)
SCALE_LOG2 = SCALE * math.log2(math.e)
MASKED = -1e30
VMEM_LIMIT = 24 * 1024 * 1024
WIDE_LIMIT = 56 * 1024 * 1024
SELECT_LIMIT = 50 * 1024 * 1024
ATTEND_LIMIT = 46 * 1024 * 1024
LOW = jnp.bfloat16


def shape_of(shape, kind=LOW):
    return jax.ShapeDtypeStruct(shape, kind)


INSIDE = pl.BlockSpec(memory_space=pltpu.VMEM)
OUTSIDE = pl.BlockSpec(memory_space=pl.ANY)


def call(kernel, name, scalars, arrays, outs, scratch=(), far_in=(), far_out=(), limit=VMEM_LIMIT):
    return pl.pallas_call(
        kernel,
        in_specs=[pl.BlockSpec(memory_space=pltpu.SMEM)] * len(scalars)
        + [OUTSIDE if i in far_in else INSIDE for i in range(len(arrays))],
        out_specs=tuple(OUTSIDE if i in far_out else INSIDE for i in range(len(outs))),
        out_shape=tuple(outs),
        scratch_shapes=list(scratch),
        compiler_params=pltpu.CompilerParams(vmem_limit_bytes=limit),
        name=name,
    )(*scalars, *arrays)


def group_columns(group):
    return pl.ds(pl.multiple_of(group * COLS, COLS), COLS)


def group_rows(group):
    return pl.ds(pl.multiple_of(group * ROWS, ROWS), ROWS)


def pack_kernel(k_ref, v_ref, tiles_ref, rows_ref, packed_ref, in_sems, out_sems):
    def fetch(part, block):
        rows = pl.ds(block * BLOCK, BLOCK)
        return pltpu.make_async_copy(
            (k_ref, v_ref)[part].at[rows, :], rows_ref.at[part, block], in_sems.at[part, block]
        )

    def ship(part, parity):
        return pltpu.make_async_copy(
            packed_ref.at[part, parity], tiles_ref.at[part, parity], out_sems.at[part, parity]
        )

    for part in range(2):
        for block in range(OWN):
            fetch(part, block).start()
    for part in range(2):
        for block in range(OWN):
            fetch(part, block).wait()
        for parity in range(PAIR):
            for group in range(GROUPS):
                for block in range(OWN):
                    packed_ref[part, parity, :, group, block] = rows_ref[
                        part, block, :, pl.ds((group * PAIR + parity) * HEAD_DIM, HEAD_DIM)
                    ].reshape(TILES, TILE, HEAD_DIM)
            ship(part, parity).start()
    for part in range(2):
        for parity in range(PAIR):
            ship(part, parity).wait()


def split_kernel(group_ref, *refs):
    for distance in range(GROUPS):
        columns = group_columns((group_ref[0] + distance) % GROUPS)
        for which in range(4):
            refs[4 + distance][which] = refs[which][:, columns]


NEAR = (4 * TOKENS + GROUPS * PAIR * TILE, COLS)


def near_parts(near_ref):
    return [near_ref.at[pl.ds(which * TOKENS, TOKENS), :] for which in range(4)]


def stats_rows(step, head):
    return pl.ds(4 * TOKENS + (step * PAIR + head) * TILE, TILE)


def pack_rows(values):
    row = lax.broadcasted_iota(jnp.int32, (TILE, ROWS), 0)
    block = jnp.zeros((TILE, ROWS), jnp.float32)
    for which, rest in enumerate(values):
        for piece in range(3):
            rounded = rest.astype(LOW).astype(jnp.float32)
            block = jnp.where(row == 3 * which + piece, rounded, block)
            rest = rest - rounded
    return block.astype(LOW)


def unpack_rows(block):
    wide = block.astype(jnp.float32)
    return [
        (wide[i + 2 : i + 3] + wide[i + 1 : i + 2]) + wide[i : i + 1] for i in (0, 3, 6)
    ]


def assemble_kernel(group_ref, *refs):
    near_ref, low_ref, high_ref = refs[GROUPS:]
    parts = near_parts(near_ref)
    for distance in range(GROUPS):
        rows = group_rows((group_ref[0] + GROUPS - distance) % GROUPS)
        for which in range(4):
            parts[which][rows, :] = refs[distance][which]
    for part in range(2):
        low_ref[part] = parts[2 + part][:BLOCK, :]
        high_ref[part] = parts[2 + part][TOKENS - BLOCK :, :]
    for step in range(GROUPS):
        for head in range(PAIR):
            scores, dprob = own_products(parts, step, head)
            top = jnp.max(scores, axis=0, keepdims=True)
            weight = jnp.exp2(scores - top)
            total = jnp.sum(weight, axis=0, keepdims=True)
            delta = jnp.sum(weight * dprob, axis=0, keepdims=True)
            near_ref[stats_rows(step, head), :] = pack_rows([top, total, delta])


CHUNK = 4


def select_kernel(random_ref, global_ref, table_ref, out_ref, chosen_ref, sems):
    common = [table_ref[global_ref[which]] for which in range(GLOBAL)]

    def ship(chunk):
        part = pl.ds(chunk * CHUNK, CHUNK)
        return pltpu.make_async_copy(chosen_ref.at[part], out_ref.at[part], sems.at[chunk])

    def fill(chunk, carry):
        for device in range(CHUNK):
            place = chunk * CHUNK + device
            for entry in range(ASKED):
                chosen_ref[place, entry] = table_ref[random_ref[place * ASKED + entry]]
            for which in range(GLOBAL):
                chosen_ref[place, ASKED + which] = common[which]
        ship(chunk).start()
        return carry

    def drain(chunk, carry):
        ship(chunk).wait()
        return carry

    lax.fori_loop(0, SEQ // CHUNK, fill, 0)
    lax.fori_loop(0, SEQ // CHUNK, drain, 0)


def dot_nt(a, b):
    return lax.dot_general(a, b, (((1,), (1,)), ((), ())), preferred_element_type=jnp.float32)


def dot_nn(a, b):
    return lax.dot_general(a, b, (((1,), (0,)), ((), ())), preferred_element_type=jnp.float32)


def dot_tn(a, b):
    return lax.dot_general(a, b, (((0,), (0,)), ((), ())), preferred_element_type=jnp.float32)


def rows_of(block):
    return slice(block * BLOCK, (block + 1) * BLOCK)


def columns_of(head):
    return pl.ds(head * HEAD_DIM, HEAD_DIM)


def step_rows(step):
    return pl.ds(pl.multiple_of(step * ROWS, ROWS), ROWS)


def edge_block(step, head, part, own_ref, prev_ref, next_ref, block):
    columns = columns_of(head)
    if step == (0, GROUPS - 1)[block]:
        return (prev_ref, next_ref)[block][part, :, columns]
    return own_ref[pl.ds(step * ROWS + (-BLOCK, ROWS)[block], BLOCK), columns]


def keysets(step, head, part, own_ref, prev_ref, next_ref, far_ref):
    def entry(index):
        return far_ref[part, head, :, index].reshape(BLOCK, HEAD_DIM)

    common = jnp.concatenate([entry(ASKED + which) for which in range(GLOBAL)], axis=0)
    private = [
        jnp.concatenate(
            [edge_block(step, head, part, own_ref, prev_ref, next_ref, block)]
            + [entry(step * STEP + block * RANDOM + r) for r in range(RANDOM)],
            axis=0,
        )
        for block in range(OWN)
    ]
    return common, private


def to_tiles(block):
    return block.astype(LOW).reshape(TILES, TILE, HEAD_DIM)


SAVED = (GROUPS, PAIR, 4 * ROWS + BLOCK + TILE, ROWS)


def saved_parts(ref):
    low, final = 3 * ROWS, 4 * ROWS + BLOCK
    return ref.at[:, :, :low, :], ref.at[:, :, low:final, :], ref.at[:, :, final:, :]


def own_products(parts, step, head):
    rows, columns = step_rows(step), columns_of(head)
    queries, grads, keys, values = (part[rows, columns] for part in parts)
    return dot_nt(keys, queries) * SCALE_LOG2, dot_nt(values, grads)


def attend_kernel(
    place_ref, near_ref, prev_in, next_in, far_ref,
    terms_out, saved_out,
    prev_ref, next_ref, terms_ref, saved_ref, edge_sems, term_sems, out_sems,
):
    place = place_ref[0]
    q_ref, d_ref, k_ref, v_ref = near_parts(near_ref)
    ds_ref, low_ref, final_ref = saved_parts(saved_ref)

    edge_copies = [
        pltpu.make_async_copy(prev_in, prev_ref, edge_sems.at[0]),
        pltpu.make_async_copy(next_in, next_ref, edge_sems.at[1]),
    ]
    for copy in edge_copies:
        copy.start()

    def ship_terms(index, start, size):
        entries = pl.ds(start, size)
        return pltpu.make_async_copy(
            terms_ref.at[:, :, :, entries], terms_out.at[:, :, :, entries], term_sems.at[index]
        )

    def ship(step):
        return [
            pltpu.make_async_copy(saved_ref.at[step], saved_out.at[step], out_sems.at[step]),
            ship_terms(step, step * STEP, STEP),
        ]

    column = lax.broadcasted_iota(jnp.int32, (1, ROWS), 1)

    def attend_head(step, head):
        queries = q_ref[step_rows(step), columns_of(head)]
        grads = d_ref[step_rows(step), columns_of(head)]
        k_common, k_private = keysets(step, head, 0, k_ref, prev_ref, next_ref, far_ref)
        v_common, v_private = keysets(step, head, 1, v_ref, prev_ref, next_ref, far_ref)
        own_max, own_total, own_delta = unpack_rows(near_ref[stats_rows(step, head), :])

        s_common = dot_nt(k_common, queries) * SCALE_LOG2
        s_private = (
            jnp.concatenate([dot_nt(k_private[b], queries[rows_of(b)]) for b in range(OWN)], axis=1)
            * SCALE_LOG2
        )
        absent = ((column < BLOCK) & (step == 0) & (place == 0)) | (
            (column >= BLOCK) & (step == GROUPS - 1) & (place == SEQ - 1)
        )
        s_edge = jnp.where(absent, MASKED, s_private[:BLOCK])
        s_random = s_private[BLOCK:]
        p_common = dot_nt(v_common, grads)
        p_private = jnp.concatenate(
            [dot_nt(v_private[b], grads[rows_of(b)]) for b in range(OWN)], axis=1
        )
        row_max = own_max
        for scores in (s_common, s_edge, s_random):
            row_max = jnp.maximum(row_max, jnp.max(scores, axis=0, keepdims=True))
        e_common = jnp.exp2(s_common - row_max)
        e_private = jnp.concatenate(
            [jnp.exp2(s_edge - row_max), jnp.exp2(s_random - row_max)], axis=0
        )
        own_scale = jnp.exp2(own_max - row_max)
        total = (
            own_total * own_scale
            + jnp.sum(e_common, axis=0, keepdims=True)
            + jnp.sum(e_private, axis=0, keepdims=True)
        )
        inverse = 1.0 / total
        delta = (
            own_delta * own_scale
            + jnp.sum(e_common * p_common, axis=0, keepdims=True)
            + jnp.sum(e_private * p_private, axis=0, keepdims=True)
        ) * inverse
        final_ref[step, head] = pack_rows([row_max, inverse, delta])

        probs_common = e_common * inverse
        probs_private = e_private * inverse
        low_private = probs_private.astype(LOW)
        ds_private = (probs_private * ((p_private - delta) * SCALE)).astype(LOW)
        low_ref[step, head, :ROWS, :] = probs_common.astype(LOW)
        low_ref[step, head, ROWS:, :] = low_private[:BLOCK]
        ds_ref[step, head, :ROWS, :] = (probs_common * ((p_common - delta) * SCALE)).astype(LOW)
        ds_ref[step, head, ROWS:, :] = ds_private

        for part, weights, other in ((0, ds_private, queries), (1, low_private, grads)):
            for block in range(OWN):
                terms = dot_nn(weights[BLOCK:, rows_of(block)], other[rows_of(block)])
                for r in range(RANDOM):
                    terms_ref[part, head, :, step * STEP + block * RANDOM + r] = to_tiles(
                        terms[rows_of(r)]
                    )

    for step in (*range(1, GROUPS - 1), 0, GROUPS - 1):
        if step == 0:
            for copy in edge_copies:
                copy.wait()
        for head in range(PAIR):
            attend_head(step, head)
        for copy in ship(step):
            copy.start()
    for part, weights_ref, other_ref in ((0, ds_ref, q_ref), (1, low_ref, d_ref)):
        for head in range(PAIR):
            total = sum(
                dot_nn(
                    weights_ref[step, head, :ROWS, :],
                    other_ref[pl.ds(step * ROWS, ROWS), columns_of(head)],
                )
                for step in range(GROUPS)
            )
            for which in range(GLOBAL):
                terms_ref[part, head, :, ASKED + which] = to_tiles(total[rows_of(which)])
            for block, step in enumerate((0, GROUPS - 1)):
                terms_ref[part, head, :, ENTRIES + block] = to_tiles(
                    dot_nn(
                        weights_ref[step, head, ROWS : ROWS + BLOCK, rows_of(block)],
                        other_ref[
                            pl.ds(step * ROWS + block * BLOCK, BLOCK), columns_of(head)
                        ],
                    )
                )
    last = ship_terms(GROUPS, ASKED, RETURNED - ASKED)
    last.start()
    for step in range(GROUPS):
        for copy in ship(step):
            copy.wait()
    last.wait()


def attend(place, near, from_prev, from_next, far):
    terms_shape = (2, PAIR, TILES, RETURNED, TILE, HEAD_DIM)
    return call(
        attend_kernel,
        "attend",
        [place],
        [near, from_prev, from_next, far.reshape((2, PAIR, TILES, ENTRIES, TILE, HEAD_DIM))],
        [shape_of(terms_shape), shape_of(SAVED)],
        [
            pltpu.VMEM((2, BLOCK, COLS), LOW),
            pltpu.VMEM((2, BLOCK, COLS), LOW),
            pltpu.VMEM(terms_shape, LOW),
            pltpu.VMEM(SAVED, LOW),
            pltpu.SemaphoreType.DMA((2,)),
            pltpu.SemaphoreType.DMA((GROUPS + 1,)),
            pltpu.SemaphoreType.DMA((GROUPS,)),
        ],
        far_in=(1, 2),
        far_out=(0, 1),
        limit=ATTEND_LIMIT,
    )


def near_kernel(
    near_ref, prev_ref, next_ref, far_ref, saved_ref, dq_ref, win_ref, sum_ref
):
    ds_ref, low_ref, final_ref = saved_parts(saved_ref)
    parts = near_parts(near_ref)
    q_ref, d_ref, k_ref, _ = parts
    sum_ref[...] = jnp.zeros_like(sum_ref)

    def near_head(step, head):
        columns = columns_of(head)
        k_common, k_private = keysets(step, head, 0, k_ref, prev_ref, next_ref, far_ref)
        row_max, inverse, delta = unpack_rows(final_ref[step, head])
        scores, dprob = own_products(parts, step, head)
        probs = jnp.exp2(scores - row_max) * inverse
        own_low = probs.astype(LOW)
        own_ds = (probs * ((dprob - delta) * SCALE)).astype(LOW)
        dq_shared = dot_tn(k_ref[step_rows(step), columns], own_ds) + dot_tn(
            k_common, ds_ref[step, head, :ROWS, :]
        )
        dq_private = jnp.concatenate(
            [dot_tn(k_private[b], ds_ref[step, head, ROWS:, rows_of(b)]) for b in range(OWN)],
            axis=1,
        )
        dq_ref[step_rows(step), columns] = (dq_shared + dq_private).T.astype(LOW)
        start = pl.multiple_of(step * ROWS, ROWS)
        for part, own_weights, weights_ref, other_ref in (
            (0, own_ds, ds_ref, q_ref),
            (1, own_low, low_ref, d_ref),
        ):
            other = other_ref[step_rows(step), columns]
            own = pl.ds(start + BLOCK, ROWS)
            sum_ref[part, own, columns] = sum_ref[part, own, columns] + dot_nn(own_weights, other)
            for block in range(OWN):
                edge = pl.ds(start + block * (BLOCK + ROWS), BLOCK)
                sum_ref[part, edge, columns] = sum_ref[part, edge, columns] + dot_nn(
                    weights_ref[step, head, ROWS : ROWS + BLOCK, rows_of(block)],
                    other[rows_of(block)],
                )

    for step in range(GROUPS):
        for head in range(PAIR):
            near_head(step, head)
    for part in range(2):
        win_ref[part] = sum_ref[part, BLOCK : BLOCK + TOKENS, :]


def near_grads(near, from_prev, from_next, far, saved):
    return call(
        near_kernel,
        "near_grads",
        [],
        [
            near, from_prev, from_next,
            far.reshape((2, PAIR, TILES, ENTRIES, TILE, HEAD_DIM)), saved,
        ],
        [
            shape_of((TOKENS, COLS)),
            shape_of((2, TOKENS, COLS), jnp.float32),
        ],
        [pltpu.VMEM((2, TOKENS + 2 * BLOCK, COLS), jnp.float32)],
    )


def collect_kernel(random_ref, global_ref, terms_in, out_ref, terms_ref, sems, *sums):
    def fetch(chunk):
        part = pl.ds(chunk * CHUNK, CHUNK)
        return pltpu.make_async_copy(terms_in.at[part], terms_ref.at[part], sems.at[chunk])

    def begin(chunk, carry):
        fetch(chunk).start()
        return carry

    lax.fori_loop(0, SEQ // CHUNK, begin, 0)
    for sum_ref in sums:
        sum_ref[...] = jnp.zeros_like(sum_ref)

    def add(which, block, device, entry):
        sum_ref = sums[which % len(sums)]
        sum_ref[block] = sum_ref[block] + terms_ref[device, entry].astype(jnp.float32)

    def step(chunk, carry):
        fetch(chunk).wait()
        for inner in range(CHUNK):
            device = chunk * CHUNK + inner
            for entry in range(ASKED):
                add(entry, random_ref[device * ASKED + entry], device, entry)
            add(0, jnp.maximum(device * LOCAL - 1, 0), device, ENTRIES)
            add(1, jnp.minimum(device * LOCAL + LOCAL, BLOCKS - 1), device, ENTRIES + 1)
            carry = tuple(
                carry[which] + terms_ref[device, ASKED + which].astype(jnp.float32)
                for which in range(GLOBAL)
            )
        return carry

    zero = jnp.zeros((TILE, HEAD_DIM), jnp.float32)
    totals = lax.fori_loop(0, SEQ // CHUNK, step, (zero,) * GLOBAL)
    for which in range(GLOBAL):
        block = global_ref[which]
        sums[0][block] = sums[0][block] + totals[which]
    result = sums[0][...]
    for sum_ref in sums[1:]:
        result = result + sum_ref[...]
    out_ref[...] = result.astype(LOW)


def regroup_kernel(group_ref, dq_ref, win_ref, *outs):
    for distance, out_ref in enumerate(outs):
        rows = group_rows((group_ref[0] + distance) % GROUPS)
        out_ref[0] = dq_ref[rows, :]
        for part in range(2):
            out_ref[1 + part] = win_ref[part, rows, :].astype(LOW)


def finish_kernel(group_ref, *refs):
    far_ref, *outs = refs[GROUPS : GROUPS + 4]
    *insides, sems = refs[GROUPS + 4 :]

    def ship(which):
        return pltpu.make_async_copy(insides[which], outs[which], sems.at[which])

    for which, inside in enumerate(insides):
        for distance in range(GROUPS):
            group = (group_ref[0] + GROUPS - distance) % GROUPS
            near_ref = refs[distance]
            if which == 0:
                inside[:, group_columns(group)] = near_ref[0]
                continue
            for parity in range(PAIR):
                columns = pl.ds(
                    pl.multiple_of(group * COLS + parity * HEAD_DIM, HEAD_DIM), HEAD_DIM
                )
                for block in range(OWN):
                    rows = pl.ds(block * BLOCK, BLOCK)
                    far = far_ref[which - 1, parity, :, group, block].reshape(BLOCK, HEAD_DIM)
                    near = near_ref[which, rows, columns_of(parity)]
                    inside[rows, columns] = (
                        near.astype(jnp.float32) + far.astype(jnp.float32)
                    ).astype(LOW)
        ship(which).start()
    for which in range(3):
        ship(which).wait()


def exchange(tiles, axes):
    return lax.all_to_all(tiles, axes, split_axis=0, concat_axis=0, tiled=True)


def around(parts):
    moved = [parts[0]]
    for distance in range(1, GROUPS):
        route = [(i, (i + distance) % GROUPS) for i in range(GROUPS)]
        moved.append(lax.ppermute(parts[distance], "head", route))
    return moved


def beside(up, down):
    forward = [(i, i + 1) for i in range(SEQ - 1)]
    backward = [(i + 1, i) for i in range(SEQ - 1)]
    return lax.ppermute(up, "seq", forward), lax.ppermute(down, "seq", backward)


def local(queries, keys, values, out_grad, random_blocks, global_blocks):
    place = lax.axis_index("seq").astype(jnp.int32).reshape(1)
    group = lax.axis_index("head").astype(jnp.int32).reshape(1)
    random_list = random_blocks.reshape(-1)
    tile_shape = (2, PAIR, TILES, GROUPS, OWN, TILE, HEAD_DIM)

    (tiles,) = call(
        pack_kernel,
        "pack_tiles",
        [],
        [keys, values],
        [shape_of(tile_shape)],
        [
            pltpu.VMEM((2, OWN, BLOCK, WIDTH), LOW),
            pltpu.VMEM(tile_shape, LOW),
            pltpu.SemaphoreType.DMA((2, OWN)),
            pltpu.SemaphoreType.DMA((2, PAIR)),
        ],
        far_in=(0, 1),
        far_out=(0,),
        limit=WIDE_LIMIT,
    )
    table = exchange(tiles.reshape(DEVICES, OWN, TILE, HEAD_DIM), AXES)
    split = call(
        split_kernel,
        "split_heads",
        [group],
        [queries, out_grad, keys, values],
        [shape_of((4, ROWS, COLS))] * GROUPS,
    )
    table, *split = lax.optimization_barrier((table, *split))
    edge_shape = shape_of((2, BLOCK, COLS))
    here, low, high = call(
        assemble_kernel,
        "assemble_heads",
        [group],
        around(split),
        [shape_of(NEAR)] + [edge_shape] * 2,
    )
    from_prev, from_next = beside(high, low)
    (chosen,) = call(
        select_kernel,
        "select_tiles",
        [random_list, global_blocks],
        [table.reshape(BLOCKS, TILE, HEAD_DIM)],
        [shape_of((SEQ, ENTRIES, TILE, HEAD_DIM))],
        [
            pltpu.VMEM((SEQ, ENTRIES, TILE, HEAD_DIM), LOW),
            pltpu.SemaphoreType.DMA((SEQ // CHUNK,)),
        ],
        far_out=(0,),
        limit=SELECT_LIMIT,
    )
    far = exchange(chosen, "seq")
    terms, saved = attend(
        place, here, from_prev, from_next, far
    )
    returned = exchange(terms.reshape(SEQ, RETURNED, TILE, HEAD_DIM), "seq")
    dq, win = near_grads(
        here, from_prev, from_next, far, saved
    )
    back_parts = call(
        regroup_kernel,
        "regroup",
        [group],
        [dq, win],
        [shape_of((3, ROWS, COLS))] * GROUPS,
    )
    near = around(back_parts)
    returned, *near = lax.optimization_barrier((returned, *near))
    (sums,) = call(
        collect_kernel,
        "collect_terms",
        [random_list, global_blocks],
        [returned],
        [shape_of((BLOCKS, TILE, HEAD_DIM))],
        [
            pltpu.VMEM((SEQ, RETURNED, TILE, HEAD_DIM), LOW),
            pltpu.SemaphoreType.DMA((SEQ // CHUNK,)),
        ]
        + [pltpu.VMEM((BLOCKS, TILE, HEAD_DIM), jnp.float32)] * 3,
        far_in=(0,),
        limit=VMEM_LIMIT,
    )
    back = exchange(sums.reshape(DEVICES, OWN, TILE, HEAD_DIM), AXES)
    return call(
        finish_kernel,
        "finish",
        [group],
        list(near) + [back.reshape(tile_shape)],
        [shape_of((ROWS, WIDTH))] * 3,
        [pltpu.VMEM((ROWS, WIDTH), LOW)] * 3 + [pltpu.SemaphoreType.DMA((3,))],
        far_out=(0, 1, 2),
    )


def solution(mesh):
    split = P(AXES, None)
    return jax.shard_map(
        local,
        mesh=mesh,
        in_specs=(split, split, split, split, P(), P()),
        out_specs=(split, split, split),
        check_vma=False,
    )
```
